256 devices in a mesh: fsdp: 64 (over x, z, core), rep: 4 (over y).
Axes of the slice: x: 4, y: 4, z: 8, core: 2. Of those that a mesh axis runs over, the one named last changes fastest.
Arguments:
- gate_shards: bfloat16 [4, 7168, 2048], P(None, 'fsdp', 'rep'), may hold values from -6 to 6
- up_shards: bfloat16 [4, 7168, 2048], P(None, 'fsdp', 'rep'), may hold values from -6 to 6
- norm_gain: float32 [7168], P('fsdp'), may hold values from 0.1 to 1.9
- matching: int32 [64], replicated, may hold values from 0 to 63, each once
- replica_slots: int32 [4, 4], replicated, may hold values from 0 to 7, as said below
- replica_count: int32 [4], replicated, may hold values from 1 to 4, as said below
Outputs:
- joined: bfloat16 [64, 7168, 512], P('fsdp')
The draws below stay inside these ranges and needn't reach their ends.
Inputs may be any that keep to these rules, and one draw needn't show every extreme that they name: `replica_slots`: every physical slot 0 to 7 appears exactly once among the first replica_count[e] entries of the rows e together; those entries of a row are ascending; the remaining entries of a row are arbitrary slots. `replica_count`: the counts sum to 8 and stay at or below 4; one expert has exactly 4 replicas in every draw. `matching`: each rank appears once.
All inputs are finite; a program needn't handle non-finite values.
Results may differ from the reference program's by a relative error of at most 0.001.
Values may be sent and summed in bfloat16 or wider, within the bound.
No kernel may reach another device: no remote copies, remote signals or barrier semaphores. Data moves between devices by JAX's collectives and lax.ppermute only.
A program may use at most 64 MiB of HBM per device.

```python
import jax
import jax.numpy as jnp

D = 7168
FF = 2048
NB = 8
FFU = 256
SLOTS = 8
E = 4
MAXREP = 4
N_FSDP = 64


def replica_tables(key):
    order = jax.random.permutation(jax.random.fold_in(key, 1), SLOTS)
    hottest = jax.random.randint(jax.random.fold_in(key, 2), (), 0, E)
    positions = jnp.arange(SLOTS, dtype=jnp.int32)
    spare = max(E - 1, 1)
    pick_other = jax.random.randint(jax.random.fold_in(key, 3), (SLOTS,), 0, spare)
    rotate = jax.random.permutation(jax.random.fold_in(key, 4), spare)
    others = (hottest + 1 + rotate[pick_other]) % E
    owner_at = jnp.where(positions < E, positions, jnp.where(positions < E + MAXREP - 1, hottest, others))
    slot_owners = jnp.zeros((SLOTS,), jnp.int32).at[order].set(owner_at.astype(jnp.int32))
    counts = jnp.sum((slot_owners[None, :] == jnp.arange(E)[:, None]).astype(jnp.int32), axis=1)
    listing = jnp.argsort(slot_owners * SLOTS + positions, stable=True).astype(jnp.int32)
    starts = jnp.cumsum(counts) - counts
    table = listing[jnp.clip(starts[:, None] + jnp.arange(MAXREP)[None, :], 0, SLOTS - 1)]
    return (table.astype(jnp.int32), counts.astype(jnp.int32))


def draw_replica_slots(key, part):
    table, counts = replica_tables(key)
    key = jax.random.fold_in(key, 7)
    filler = jax.random.randint(key, (E, MAXREP), 0, SLOTS)
    live = jnp.arange(MAXREP)[None, :] < counts[:, None]
    return jnp.where(live, table, filler).astype(jnp.int32)


def draw_replica_count(key, part):
    table, counts = replica_tables(key)
    return counts.astype(jnp.int32)


def shard_levels(rng, extent, cuts, low, largest):
    def one(dim, parts):
        draws = jax.random.uniform(jax.random.fold_in(jax.random.fold_in(rng, 6), dim), (parts,), jnp.float32, low / len(cuts), largest / len(cuts))
        return jnp.repeat(jnp.exp(draws), extent[dim] // parts).reshape((-1,) + (1,) * (len(extent) - dim - 1))

    level = one(*cuts[0])
    for cut in cuts[1:]:
        level = level * one(*cut)
    return level


def scatter_about(stream_key, shape, spread, most, cuts=(), kind=jnp.bfloat16):
    factor_of = shard_levels(stream_key, shape, cuts, -0.22, 0.18) if cuts else 1.0
    result = jax.random.normal(stream_key, shape, jnp.float32) * spread * factor_of
    return jnp.minimum(jnp.maximum(result, -most), most).astype(kind)


def setup_inputs(seed: int = 0) -> dict:
    key_of = jax.random.split(jax.random.key(seed), 7)
    gate_shards = scatter_about(key_of[0], (E, D, FF), 1.0, 6.0, ((1, 64), (2, 4)))
    up_shards = scatter_about(key_of[1], (E, D, FF), 1.0, 6.0, ((1, 64), (2, 4)))
    norm_gain = jnp.clip(1.0 + 0.18 * jax.random.normal(key_of[2], (D,), jnp.float32), 0.1, 1.9)
    matching = jax.random.permutation(key_of[3], N_FSDP).astype(jnp.int32)
    replica_slots = draw_replica_slots(jax.random.fold_in(key_of[6], 71), 0)
    replica_count = draw_replica_count(jax.random.fold_in(key_of[6], 71), 0)
    return dict(gate_shards=gate_shards, up_shards=up_shards, norm_gain=norm_gain, matching=matching, replica_slots=replica_slots, replica_count=replica_count)


def slot_owner(replica_slots, replica_count, slots):
    live = jnp.arange(replica_slots.shape[1])[None, :] < replica_count[:, None]
    hits = live[:, :, None] & (replica_slots[:, :, None] == jnp.arange(slots)[None, None, :])
    owners = jnp.arange(replica_slots.shape[0], dtype=jnp.int32)[:, None, None] * hits.astype(jnp.int32)
    return jnp.sum(owners, axis=(0, 1)).astype(jnp.int32)


def inverse_order(matching):
    count = matching.shape[0]
    match_grid = matching[None, :] == jnp.arange(count, dtype=jnp.int32)[:, None]
    ranks = jnp.where(match_grid, jnp.arange(count, dtype=jnp.int32)[None, :], 0)
    return jnp.sum(ranks, axis=1).astype(jnp.int32)


def reference(gate_shards, up_shards, norm_gain, matching, replica_slots, replica_count):
    rows = D // N_FSDP
    owners = slot_owner(replica_slots, replica_count, SLOTS)
    targets = jnp.arange(N_FSDP, dtype=jnp.int32)
    expert_pick = owners[targets // NB]
    block_pick = targets % NB
    inverse = inverse_order(matching)
    gate_model = gate_shards.reshape(E, N_FSDP, rows, FF)[:, inverse].reshape(E, D, FF)
    up_model = up_shards.reshape(E, N_FSDP, rows, FF)[:, inverse].reshape(E, D, FF)
    gain_model = norm_gain.reshape(N_FSDP, rows)[inverse].reshape(D)
    gate_pick = gate_model.reshape(E, D, FFU, NB)[expert_pick, :, :, block_pick]
    up_pick = up_model.reshape(E, D, FFU, NB)[expert_pick, :, :, block_pick]
    gate_fold = (gate_pick.astype(jnp.float32) * gain_model[None, :, None]).astype(jnp.bfloat16)
    up_fold = (up_pick.astype(jnp.float32) * gain_model[None, :, None]).astype(jnp.bfloat16)
    return jnp.stack((gate_fold, up_fold), axis=-1).reshape(N_FSDP, D, 2 * FFU)
```

```python
import functools

import jax
import jax.numpy as jnp
from jax import lax
from jax.experimental import pallas as pl
from jax.experimental.pallas import tpu as pltpu
from jax.sharding import PartitionSpec as P

NX, NZ, NY = 4, 8, 4
SLOTS, BLOCKS = 8, 8
GROUPS = ((0,), (1, 7), (2, 6, 3, 5, 4))
CLASSES = ((0,), (1, 7), (2, 6), (3, 5), (4,))
BF16 = jnp.bfloat16


def place():
    me = lax.axis_index("fsdp")
    return me // (2 * NZ), (me // 2) % NZ, me % 2


def pick_matrix(core):
    unit = lax.broadcasted_iota(jnp.int32, (1024, 512), 0)
    column = lax.broadcasted_iota(jnp.int32, (1024, 512), 1)
    lane = column % 128
    wanted = (lane % 2) * 512 + 8 * (lane // 2) + 2 * (column // 128) + core
    return (unit == wanted).astype(BF16)


def prepare_kernel(slots_ref, count_ref, gate, up, gate_far, up_far, gain, gain_far, matrix, *rest):
    outs, (picked, owner) = rest[:-2], rest[-2:]
    experts, rows = gate.shape[:2]
    x, z, _ = place()
    for e in range(experts):
        for k in range(slots_ref.shape[1]):
            @pl.when(k < count_ref[e])
            def _():
                owner[slots_ref[e, k]] = e
    for side, (g, u, scale) in enumerate(((gate, up, gain), (gate_far, up_far, gain_far))):
        for e in range(experts):
            got = jnp.dot(g[e], matrix[:512, :], preferred_element_type=jnp.float32)
            got += jnp.dot(u[e], matrix[512:, :], preferred_element_type=jnp.float32)
            got = (got * scale[...]).astype(BF16)
            for zl in range(4):
                picked[e * 4 + zl, side] = got[:, zl * 128 : (zl + 1) * 128]
    for g, group in enumerate(GROUPS):
        for k, dz in enumerate(group):
            zt = (z + dz) % NZ
            for dx in range(NX):
                xt = (x + dx) % NX
                source = owner[xt * 2 + zt // 4] * 4 + zt % 4
                outs[g * NX + dx][k] = picked[source]


def prepare(gate, up, gain, matrix, replica_slots, replica_count):
    rows = gate.shape[1]
    flip = [(i, i ^ 1) for i in range(2 * NX * NZ)]
    gate_far = lax.ppermute(gate, "fsdp", flip)
    up_far = lax.ppermute(up, "fsdp", flip)
    gain_far = lax.ppermute(gain, "fsdp", flip)
    shapes = [
        jax.ShapeDtypeStruct((len(group), 2, rows, 128), BF16) for group in GROUPS for _ in range(NX)
    ]
    vmem = pl.BlockSpec(memory_space=pltpu.VMEM)
    smem = pl.BlockSpec(memory_space=pltpu.SMEM)
    outs = pl.pallas_call(
        prepare_kernel,
        out_shape=shapes,
        in_specs=[smem, smem] + [vmem] * 7,
        out_specs=[vmem] * len(shapes),
        scratch_shapes=[pltpu.VMEM((16, 2, rows, 128), BF16), pltpu.SMEM((SLOTS,), jnp.int32)],
        compiler_params=pltpu.CompilerParams(vmem_limit_bytes=32 * 1024 * 1024),
        name="prepare",
    )(
        replica_slots, replica_count, gate, up, gate_far, up_far,
        gain.reshape(rows, 1), gain_far.reshape(rows, 1), matrix,
    )
    return [outs[g * NX : (g + 1) * NX] for g in range(len(GROUPS))]


def place_kernel(dzs, base, matching, *refs):
    n = len(dzs)
    own, (left, right, far_left, far_right) = refs[:n], refs[n : n + 4]
    out, held, built, load_sems, save_sems = refs[-5:]
    count, rows = 8 * n, own[0].shape[1]
    half = count // 2
    x, z, core = place()
    y = lax.axis_index("rep")
    sources = [(0, 8 * k, ref.at[pl.ds(0, 8)]) for k, ref in enumerate(own)]
    sources += [
        (3, 0, left.at[pl.ds(0, count)]),
        (1, 0, right.at[pl.ds(0, count)]),
        (2, 0, far_left.at[pl.ds(base, half)]),
        (2, half, far_right.at[pl.ds(base, half)]),
    ]
    loads = []
    for step, at, ref in sources:
        load = pltpu.make_async_copy(
            ref, held.at[step, pl.ds(at, ref.shape[0])], load_sems.at[len(loads)]
        )
        load.start()
        loads.append(load)
    for load in loads:
        load.wait()
    saves = []
    for k, dz in enumerate(dzs):
        for dx in range(NX):
            for side in range(2):
                at = (k * NX + dx) * 2 + side
                for step in range(NY):
                    column = pl.multiple_of(((y + step) % NY) * 128, 128)
                    built[at, :, pl.ds(column, 128)] = held[step, at]
                block = matching[(((x - dx) % NX) * NZ + (z - dz) % NZ) * 2 + (core ^ side)]
                row = pl.multiple_of(block * rows, 16)
                save = pltpu.make_async_copy(built.at[at], out.at[pl.ds(row, rows)], save_sems.at[at])
                save.start()
                saves.append(save)
    for save in saves:
        save.wait()


def place_class(dzs, base, out, matching, own, left, right, far_left, far_right, devices):
    rows = own[0].shape[1]
    n = len(dzs)
    anywhere = pl.BlockSpec(memory_space=pl.ANY)
    args = [matching, *own, left, right, far_left, far_right] + ([] if out is None else [out])
    return pl.pallas_call(
        functools.partial(place_kernel, dzs, base),
        out_shape=jax.ShapeDtypeStruct((devices * rows, 512), BF16),
        in_specs=[pl.BlockSpec(memory_space=pltpu.SMEM)] + [anywhere] * (len(args) - 1),
        out_specs=anywhere,
        scratch_shapes=[
            pltpu.VMEM((NY, 8 * n, rows, 128), BF16),
            pltpu.VMEM((8 * n, rows, 512), BF16),
            pltpu.SemaphoreType.DMA((n + 4,)),
            pltpu.SemaphoreType.DMA((8 * n,)),
        ],
        input_output_aliases={} if out is None else {len(args) - 1: 0},
        compiler_params=pltpu.CompilerParams(vmem_limit_bytes=16 * 1024 * 1024),
        name="place",
    )(*args)


def local(gate, up, norm_gain, matching, replica_slots, replica_count):
    devices = lax.axis_size("fsdp")
    rows = gate.shape[1]
    _, _, core = place()
    matrix = pick_matrix(core)
    parts = prepare(gate, up, norm_gain, matrix, replica_slots, replica_count)

    def along_x(dx):
        return [(i, ((i // 16 + dx) % NX) * 16 + i % 16) for i in range(devices)]

    def along_z(dz):
        return [(i, (i // 16) * 16 + ((i // 2 + dz) % NZ) * 2 + i % 2) for i in range(devices)]

    def along_y(dy):
        return [(i, (i + dy) % NY) for i in range(NY)]

    ready = {}
    for group, pieces in zip(GROUPS, parts):
        arrived = [pieces[0]] + [lax.ppermute(pieces[dx], "fsdp", along_x(dx)) for dx in range(1, NX)]
        for k, dz in enumerate(group):
            own = jnp.stack([a[k] for a in arrived]).reshape(8, rows, 128)
            ready[dz] = lax.ppermute(own, "fsdp", along_z(dz)) if dz else own

    out = None
    left, right, owns = [], [], []
    for step in range(len(CLASSES) + 2):
        to_right, to_left = [], []
        if step < len(CLASSES):
            owns.append([ready[dz] for dz in CLASSES[step]])
            to_right += owns[step]
            to_left += owns[step]
        base = sum(p.shape[0] for p in to_right)
        if step >= 2:
            count = 8 * len(CLASSES[step - 2])
            to_right.append(left[step - 2][: count // 2])
            to_left.append(right[step - 2][count // 2 : count])
        left.append(lax.ppermute(jnp.concatenate(to_right), "rep", along_y(1)))
        right.append(lax.ppermute(jnp.concatenate(to_left), "rep", along_y(-1)))
        if step >= 2:
            k = step - 2
            out = place_class(
                CLASSES[k], base, out, matching, owns[k], left[k], right[k], left[step], right[step], devices
            )
    return out[None]


def solution(mesh):
    return jax.shard_map(
        local,
        mesh=mesh,
        in_specs=(P(None, "fsdp", "rep"), P(None, "fsdp", "rep"), P("fsdp"), P(), P(), P()),
        out_specs=P("fsdp", None, None),
        check_vma=False,
    )
```

```python
import functools

import jax
import jax.numpy as jnp
from jax import lax
from jax.experimental import pallas as pl
from jax.experimental.pallas import tpu as pltpu
from jax.sharding import PartitionSpec as P

NX, NZ, NY = 4, 8, 4
SLOTS, BLOCKS = 8, 8
GROUPS = ((1, 7), (3, 5))
BF16 = jnp.bfloat16


def place():
    me = lax.axis_index("fsdp")
    return me // (2 * NZ), (me // 2) % NZ, me % 2


def after(arrays, *done):
    return lax.optimization_barrier((list(arrays), done))[0]


def pick_matrix(core):
    unit = lax.broadcasted_iota(jnp.int32, (1024, 512), 0)
    column = lax.broadcasted_iota(jnp.int32, (1024, 512), 1)
    lane = column % 128
    wanted = (lane % 2) * 512 + 8 * (lane // 2) + 2 * (column // 128) + core
    return (unit == wanted).astype(BF16)


def prepare_kernel(tables, *refs):
    sources, (gain, gain_far, matrix), outs = refs[:4], refs[4:7], refs[7:-2]
    picked, owner = refs[-2:]
    experts, rows = sources[0].shape[:2]
    x, z, _ = place()
    for e in range(experts):
        for k in range(4):
            @pl.when(k < tables[16 + e])
            def _():
                owner[tables[4 * e + k]] = e
    for side, scale in enumerate((gain, gain_far)):
        for e in range(experts):
            got = jnp.dot(sources[2 * side][e], matrix[:512, :], preferred_element_type=jnp.float32)
            got += jnp.dot(sources[2 * side + 1][e], matrix[512:, :], preferred_element_type=jnp.float32)
            got = (got * scale[...]).astype(BF16)
            for zl in range(4):
                picked[e * 4 + zl, side] = got[:, zl * 128 : (zl + 1) * 128]
    for g, group in enumerate(GROUPS):
        for k, dz in enumerate(group):
            zt = (z + dz) % NZ
            for dx in range(NX):
                xt = (x + dx) % NX
                source = owner[xt * 2 + zt // 4] * 4 + zt % 4
                outs[g * NX + dx][k] = picked[source]
    for xt in range(NX):
        for k in range(NZ // 2):
            zt = 2 * k + z % 2
            outs[-1][xt * (NZ // 2) + k] = picked[owner[xt * 2 + zt // 4] * 4 + zt % 4]


def prepare(gate, up, gain, matrix, tables):
    rows = gate.shape[1]
    flip = [(i, i ^ 1) for i in range(2 * NX * NZ)]
    gate_far = lax.ppermute(gate, "fsdp", flip)
    up_far = lax.ppermute(up, "fsdp", flip)
    gain_far = lax.ppermute(gain, "fsdp", flip)
    shapes = [
        jax.ShapeDtypeStruct((len(group), 2, rows, 128), BF16) for group in GROUPS for _ in range(NX)
    ] + [jax.ShapeDtypeStruct((NX * NZ // 2, 2, rows, 128), BF16)]
    vmem = pl.BlockSpec(memory_space=pltpu.VMEM)
    smem = pl.BlockSpec(memory_space=pltpu.SMEM)
    outs = pl.pallas_call(
        prepare_kernel,
        out_shape=shapes,
        in_specs=[smem] + [vmem] * 7,
        out_specs=[vmem] * len(shapes),
        scratch_shapes=[
            pltpu.VMEM((16, 2, rows, 128), BF16),
            pltpu.SMEM((SLOTS,), jnp.int32),
        ],
        compiler_params=pltpu.CompilerParams(vmem_limit_bytes=16 * 1024 * 1024),
        name="prepare",
    )(
        tables, gate, up, gate_far, up_far,
        gain.reshape(rows, 1), gain_far.reshape(rows, 1), matrix,
    )
    return [outs[g * NX : (g + 1) * NX] for g in range(len(GROUPS))], outs[-1]


def place_kernel(blocks, sizes, relative, tables, *refs):
    held = refs[-len(sizes) - 3 : -3]
    built, load_sems, save_sems = refs[-3:]
    out, rows = refs[-len(sizes) - 4], built.shape[1]
    x, z, core = place()
    y = lax.axis_index("rep")
    loads = [
        pltpu.make_async_copy(refs[k].at[pl.ds(at, size)], held[k], load_sems.at[k])
        for k, (at, size) in enumerate(sizes)
    ]
    for load in loads:
        load.start()
    for load in loads:
        load.wait()
    saves = []
    for at, (dz, dx, side, parts) in enumerate(blocks):
        for step, (k, index) in enumerate(parts):
            group = (y + step) % NY if relative else step
            built[at, :, pl.ds(pl.multiple_of(group * 128, 128), 128)] = held[k][index]
        xs, zs = ((x - dx) % NX, (z - dz) % NZ) if dz is not None else (dx // 4, 2 * (dx % 4) + z % 2)
        block = tables[20 + (xs * NZ + zs) * 2 + (core ^ side)]
        row = pl.multiple_of(block * rows, 16)
        save = pltpu.make_async_copy(built.at[at], out.at[pl.ds(row, rows)], save_sems.at[at])
        save.start()
        saves.append(save)
    for save in saves:
        save.wait()


def place_blocks(out, tables, devices, arrays, blocks, relative=True):
    rows = arrays[0][0].shape[1]
    anywhere = pl.BlockSpec(memory_space=pl.ANY)
    sizes = [(at, size) for _, at, size in arrays]
    args = [tables] + [array for array, _, _ in arrays] + ([] if out is None else [out])
    total = len(blocks) * rows * 512 * 2
    return pl.pallas_call(
        functools.partial(place_kernel, blocks, sizes, relative),
        out_shape=jax.ShapeDtypeStruct((devices * rows, 512), BF16),
        in_specs=[pl.BlockSpec(memory_space=pltpu.SMEM)] + [anywhere] * (len(args) - 1),
        out_specs=anywhere,
        scratch_shapes=[pltpu.VMEM((size, rows, 128), BF16) for _, size in sizes]
        + [
            pltpu.VMEM((len(blocks), rows, 512), BF16),
            pltpu.SemaphoreType.DMA((len(sizes),)),
            pltpu.SemaphoreType.DMA((len(blocks),)),
        ],
        input_output_aliases={} if out is None else {len(args) - 1: 0},
        compiler_params=pltpu.CompilerParams(vmem_limit_bytes=16 * 1024 * 1024),
        cost_estimate=pl.CostEstimate(flops=0, bytes_accessed=2 * total, transcendentals=0),
        name="place",
    )(*args)


def local(gate, up, norm_gain, matching, replica_slots, replica_count):
    devices = lax.axis_size("fsdp")
    rows = gate.shape[1]
    _, _, core = place()
    matrix = pick_matrix(core)
    tables = jnp.concatenate([replica_slots.reshape(16), replica_count, matching])
    parts, even = prepare(gate, up, norm_gain, matrix, tables)

    def along_x(dx):
        return [(i, ((i // 16 + dx) % NX) * 16 + i % 16) for i in range(devices)]

    def along_z(dz):
        return [(i, (i // 16) * 16 + ((i // 2 + dz) % NZ) * 2 + i % 2) for i in range(devices)]

    def along_y(dy):
        return [(i, (i + dy) % NY) for i in range(NY)]

    same_parity = [
        [(x * NZ + 2 * k + odd) * 2 + c for x in range(NX) for k in range(NZ // 2)]
        for odd in range(2) for c in range(2)
    ]

    def cross_x(g, *done):
        pieces = after(parts[g], *done)
        got = [pieces[0]] + [lax.ppermute(pieces[dx], "fsdp", along_x(dx)) for dx in range(1, NX)]
        return [jnp.stack([a[k] for a in got]).reshape(8, rows, 128) for k in range(len(GROUPS[g]))]

    def cross_z(dzs, pieces, *done):
        pieces = after(pieces, *done)
        return [lax.ppermute(p, "fsdp", along_z(dz)) for dz, p in zip(dzs, pieces)]

    def cross_y(to_right, to_left, *done):
        pair = after([jnp.concatenate(to_right), jnp.concatenate(to_left)], *done)
        return lax.ppermute(pair[0], "rep", along_y(1)), lax.ppermute(pair[1], "rep", along_y(-1))

    def ring_blocks(dzs):
        n, count = len(dzs), 8 * len(dzs)
        blocks = []
        for at in range(count):
            dz, dx, side = dzs[at // 8], at % 8 // 2, at % 2
            far = (n + 2, at) if at < count // 2 else (n + 3, at - count // 2)
            blocks.append((dz, dx, side, ((at // 8, at % 8), (n + 1, at), far, (n, at))))
        return blocks

    def finish(out, dzs, own, left, right, far_left, far_right, base):
        count = 8 * len(dzs)
        arrays = [(a, 0, 8) for a in own]
        arrays += [(left, 0, count), (right, 0, count)]
        arrays += [(far_left, base, count // 2), (far_right, base, count // 2)]
        return place_blocks(out, tables, devices, arrays, ring_blocks(dzs))

    own1 = cross_z((1, 7), [jnp.concatenate([piece[k] for piece in parts[0]]) for k in range(2)])
    own = lax.all_to_all(even, "fsdp", 0, 0, tiled=True, axis_index_groups=same_parity)
    own = own.reshape(32, rows, 128)
    l1, r1 = cross_y(own1, own1)
    h1 = cross_y([l1[:8]], [r1[8:16]])
    le, re = cross_y([own], [own], *h1)
    bundles = []
    for dx in range(NX):
        here = [slice(8 * k + 2 * dx, 8 * k + 2 * dx + 2) for k in range(2)]
        bundle = [own1[k][here[0]] for k in range(2)] + [r1[h] for h in here]
        bundle += [h1[0][here[0]], h1[1][here[0]]] + [l1[h] for h in here]
        bundle = jnp.concatenate(bundle)
        bundles.append(lax.ppermute(bundle, "fsdp", along_x(dx)) if dx else bundle)
    own3 = cross_z((3, 5), cross_x(1, *own1))
    l3, r3 = cross_y(own3 + [le[:16]], own3 + [re[16:]])
    late = [
        (dz, dx, side, tuple((dx, step * 4 + 2 * k + side) for step in range(NY)))
        for dx in range(NX) for k, dz in enumerate(GROUPS[0]) for side in range(2)
    ]
    out = place_blocks(None, tables, devices, [(b, 0, 16) for b in bundles], late)
    l4, r4 = cross_y([l3[:8]], [r3[8:16]])
    evens = [
        (None, at // 2, at % 2, ((0, at), (2, at), (3, at) if at < 16 else (4, at - 16), (1, at)))
        for at in range(32)
    ]
    arrays = [(own, 0, 32), (le, 0, 32), (re, 0, 32), (l3, 16, 16), (r3, 16, 16)]
    out = place_blocks(out, tables, devices, arrays, evens)
    out = finish(out, (3, 5), own3, l3, r3, l4, r4, 0)
    return out[None]


def solution(mesh):
    return jax.shard_map(
        local,
        mesh=mesh,
        in_specs=(P(None, "fsdp", "rep"), P(None, "fsdp", "rep"), P("fsdp"), P(), P(), P()),
        out_specs=P("fsdp", None, None),
        check_vma=False,
    )
```

```python
import functools

import jax
import jax.numpy as jnp
from jax import lax
from jax.experimental import pallas as pl
from jax.experimental.pallas import tpu as pltpu
from jax.sharding import PartitionSpec as P

NX, NZ, NY = 4, 8, 4
SLOTS, BLOCKS = 8, 8
GROUPS = ((1, 7), (3, 5))
BF16 = jnp.bfloat16


def place():
    me = lax.axis_index("fsdp")
    return me // (2 * NZ), (me // 2) % NZ, me % 2


def after(arrays, *done):
    return lax.optimization_barrier((list(arrays), done))[0]


def pick_matrix(core):
    unit = lax.broadcasted_iota(jnp.int32, (1024, 512), 0)
    column = lax.broadcasted_iota(jnp.int32, (1024, 512), 1)
    lane = column % 128
    wanted = (lane % 2) * 512 + 8 * (lane // 2) + 2 * (column // 128) + core
    return (unit == wanted).astype(BF16)


def prepare_kernel(tables, *refs):
    sources, (gain, gain_far, matrix), outs = refs[:4], refs[4:7], refs[7:-2]
    picked, owner = refs[-2:]
    experts, rows = sources[0].shape[:2]
    x, z, _ = place()
    for e in range(experts):
        for k in range(4):
            @pl.when(k < tables[16 + e])
            def _():
                owner[tables[4 * e + k]] = e
    for side, scale in enumerate((gain, gain_far)):
        gate, up = (ref[...].reshape(experts * rows, 512) for ref in sources[2 * side : 2 * side + 2])
        got = jnp.dot(gate, matrix[:512, :], preferred_element_type=jnp.float32)
        got += jnp.dot(up, matrix[512:, :], preferred_element_type=jnp.float32)
        for e in range(experts):
            part = (got[e * rows : (e + 1) * rows] * scale[...]).astype(BF16)
            for zl in range(4):
                picked[e * 4 + zl, side] = part[:, zl * 128 : (zl + 1) * 128]
    for g, group in enumerate(GROUPS):
        for k, dz in enumerate(group):
            zt = (z + dz) % NZ
            for dx in range(NX):
                xt = (x + dx) % NX
                source = owner[xt * 2 + zt // 4] * 4 + zt % 4
                outs[g * NX + dx][k] = picked[source]
    for xt in range(NX):
        for k in range(NZ // 2):
            zt = 2 * k + z % 2
            outs[-1][xt * (NZ // 2) + k] = picked[owner[xt * 2 + zt // 4] * 4 + zt % 4]


def prepare(gate, up, gain, matrix, tables):
    rows = gate.shape[1]
    flip = [(i, i ^ 1) for i in range(2 * NX * NZ)]
    gate_far = lax.ppermute(gate, "fsdp", flip)
    up_far = lax.ppermute(up, "fsdp", flip)
    gain_far = lax.ppermute(gain, "fsdp", flip)
    shapes = [
        jax.ShapeDtypeStruct((len(group), 2, rows, 128), BF16) for group in GROUPS for _ in range(NX)
    ] + [jax.ShapeDtypeStruct((NX * NZ // 2, 2, rows, 128), BF16)]
    vmem = pl.BlockSpec(memory_space=pltpu.VMEM)
    smem = pl.BlockSpec(memory_space=pltpu.SMEM)
    outs = pl.pallas_call(
        prepare_kernel,
        out_shape=shapes,
        in_specs=[smem] + [vmem] * 7,
        out_specs=[vmem] * len(shapes),
        scratch_shapes=[
            pltpu.VMEM((16, 2, rows, 128), BF16),
            pltpu.SMEM((SLOTS,), jnp.int32),
        ],
        compiler_params=pltpu.CompilerParams(vmem_limit_bytes=16 * 1024 * 1024),
        name="prepare",
    )(
        tables, gate, up, gate_far, up_far,
        gain.reshape(rows, 1), gain_far.reshape(rows, 1), matrix,
    )
    return [outs[g * NX : (g + 1) * NX] for g in range(len(GROUPS))], outs[-1]


def cost(megabytes):
    return pl.CostEstimate(flops=0, bytes_accessed=int(megabytes * 1e6), transcendentals=0)


def pack_kernel(outs, count, *refs):
    for out, entries in zip(refs[count:], outs):
        for at, (k, index) in enumerate(entries):
            out[at] = refs[k][index]


def pack(arrays, outs):
    vmem = pl.BlockSpec(memory_space=pltpu.VMEM)
    return pl.pallas_call(
        functools.partial(pack_kernel, outs, len(arrays)),
        out_shape=[jax.ShapeDtypeStruct((len(out),) + arrays[0].shape[1:], BF16) for out in outs],
        in_specs=[vmem] * len(arrays),
        out_specs=[vmem] * len(outs),
        compiler_params=pltpu.CompilerParams(vmem_limit_bytes=16 * 1024 * 1024),
        cost_estimate=cost(1),
        name="pack",
    )(*arrays)


def blocks_of(array, start, stop):
    return [(array, index) for index in range(start, stop)]


def place_kernel(blocks, arrays, tables, *refs):
    held = refs[:arrays]
    out, built, sems = refs[-3:]
    rows = built.shape[1]
    x, z, core = place()
    y = lax.axis_index("rep")
    saves = []
    for at, (dz, side, xs, dx, parts) in enumerate(blocks):
        for step, (k, index) in enumerate(parts):
            column = pl.multiple_of(((y + step) % NY) * 128, 128)
            built[at, :, pl.ds(column, 128)] = held[k][index]
        if dx is None:
            source = xs * NZ + (2 * dz + z % 2)
        else:
            source = (x - dx) % NX * NZ + (z - dz) % NZ
        block = tables[20 + source * 2 + (core ^ side)]
        row = pl.multiple_of(block * rows, 16)
        save = pltpu.make_async_copy(built.at[at], out.at[pl.ds(row, rows)], sems.at[at])
        save.start()
        saves.append(save)
    for save in saves:
        save.wait()


def place_blocks(out, tables, devices, arrays, blocks):
    rows = arrays[0].shape[1]
    vmem, anywhere = pl.BlockSpec(memory_space=pltpu.VMEM), pl.BlockSpec(memory_space=pl.ANY)
    args = [tables, *arrays] + ([] if out is None else [out])
    total = len(blocks) * rows * 512 * 2
    return pl.pallas_call(
        functools.partial(place_kernel, blocks, len(arrays)),
        out_shape=jax.ShapeDtypeStruct((devices * rows, 512), BF16),
        in_specs=[pl.BlockSpec(memory_space=pltpu.SMEM)] + [vmem] * len(arrays)
        + ([] if out is None else [anywhere]),
        out_specs=anywhere,
        scratch_shapes=[
            pltpu.VMEM((len(blocks), rows, 512), BF16),
            pltpu.SemaphoreType.DMA((len(blocks),)),
        ],
        input_output_aliases={} if out is None else {len(args) - 1: 0},
        compiler_params=pltpu.CompilerParams(vmem_limit_bytes=24 * 1024 * 1024),
        cost_estimate=cost(2e-6 * total),
        name="place",
    )(*args)


def local(gate, up, norm_gain, matching, replica_slots, replica_count):
    devices = lax.axis_size("fsdp")
    rows = gate.shape[1]
    _, _, core = place()
    matrix = pick_matrix(core)
    tables = jnp.concatenate([replica_slots.reshape(16), replica_count, matching])
    parts, even = prepare(gate, up, norm_gain, matrix, tables)

    def along_x(dx):
        return [(i, ((i // 16 + dx) % NX) * 16 + i % 16) for i in range(devices)]

    def along_z(dz):
        return [(i, (i // 16) * 16 + ((i // 2 + dz) % NZ) * 2 + i % 2) for i in range(devices)]

    def along_y(dy):
        return [(i, (i + dy) % NY) for i in range(NY)]

    same_parity = [
        [(x * NZ + 2 * k + odd) * 2 + c for x in range(NX) for k in range(NZ // 2)]
        for odd in range(2) for c in range(2)
    ]

    def cross_x(g, *done):
        pieces = after(parts[g], *done)
        got = [pieces[0]] + [lax.ppermute(pieces[dx], "fsdp", along_x(dx)) for dx in range(1, NX)]
        return [jnp.stack([a[k] for a in got]).reshape(8, rows, 128) for k in range(len(GROUPS[g]))]

    def cross_z(dzs, pieces, *done):
        pieces = after(pieces, *done)
        return [lax.ppermute(p, "fsdp", along_z(dz)) for dz, p in zip(dzs, pieces)]

    def cross_y(to_right, to_left, *done):
        pair = after([jnp.concatenate(to_right), jnp.concatenate(to_left)], *done)
        return lax.ppermute(pair[0], "rep", along_y(1)), lax.ppermute(pair[1], "rep", along_y(-1))

    own1 = cross_z((1, 7), [jnp.concatenate([piece[k] for piece in parts[0]]) for k in range(2)])
    own = lax.all_to_all(even, "fsdp", 0, 0, tiled=True, axis_index_groups=same_parity)
    own = own.reshape(32, rows, 128)
    l1, r1 = cross_y(own1, own1)
    h1 = cross_y([l1[:8]], [r1[8:16]])
    le, re = cross_y([own], [own], *h1)
    bundles = []
    for dx in range(NX):
        here = [slice(8 * k + 2 * dx, 8 * k + 2 * dx + 2) for k in range(2)]
        bundle = [own1[k][here[0]] for k in range(2)] + [r1[h] for h in here]
        bundle += [h1[0][here[0]], h1[1][here[0]]] + [l1[h] for h in here]
        bundle = jnp.concatenate(bundle)
        bundles.append(lax.ppermute(bundle, "fsdp", along_x(dx)) if dx else bundle)
    own3 = cross_z((3, 5), cross_x(1, *own1))
    l3, r3 = cross_y(own3 + [le[:16]], own3 + [re[16:]])
    l4, r4 = cross_y([l3[:8]], [r3[8:16]])
    late = [
        (dz, side, None, dx, tuple((dx, step * 4 + 2 * k + side) for step in range(NY)))
        for dx in range(NX) for k, dz in enumerate(GROUPS[0]) for side in range(2)
    ]
    out = place_blocks(None, tables, devices, bundles, late)
    evens = [
        (at // 2 % 4, at % 2, at // 8, None, ((0, at), (2, at), (3, 16 + at) if at < 16 else (4, at), (1, at)))
        for at in range(32)
    ]
    out = place_blocks(out, tables, devices, [own, le, re, l3, r3], evens)
    odds = [
        (GROUPS[1][at // 8], at % 2, None, at % 8 // 2,
         ((at // 8, at % 8), (3, at), (4, at) if at < 8 else (5, at - 8), (2, at)))
        for at in range(16)
    ]
    out = place_blocks(out, tables, devices, [*own3, l3, r3, l4, r4], odds)
    return out[None]


def solution(mesh):
    return jax.shard_map(
        local,
        mesh=mesh,
        in_specs=(P(None, "fsdp", "rep"), P(None, "fsdp", "rep"), P("fsdp"), P(), P(), P()),
        out_specs=P("fsdp", None, None),
        check_vma=False,
    )
```

```python
import functools

import jax
import jax.numpy as jnp
from jax import lax
from jax.experimental import pallas as pl
from jax.experimental.pallas import tpu as pltpu
from jax.sharding import PartitionSpec as P

NX, NZ, NY = 4, 8, 4
SLOTS, BLOCKS = 8, 8
GROUPS = ((1, 7), (3, 5))
BF16 = jnp.bfloat16


def place():
    me = lax.axis_index("fsdp")
    return me // (2 * NZ), (me // 2) % NZ, me % 2


def after(arrays, *done):
    return lax.optimization_barrier((list(arrays), done))[0]


def slot_owner(replica_slots, replica_count):
    shape = (SLOTS,) + replica_slots.shape
    slot, expert, place_in_list = (lax.broadcasted_iota(jnp.int32, shape, k) for k in range(3))
    live = jnp.clip(replica_count[None, :, None] - place_in_list, 0, 1)
    return jnp.sum(jnp.where(replica_slots[None] == slot, live * expert, 0), axis=(1, 2))


def pick_matrix(core):
    shape = (2, 512, 256)
    half, row, column = (lax.broadcasted_iota(jnp.int32, shape, k) for k in range(3))
    lane = column % 64
    residue = (column // 64) ^ half
    wanted = (lane % 2) * 256 + 8 * (lane // 2) + 2 * residue + core
    return (row == wanted).astype(BF16)


def fold_rows(weights, gain):
    return (weights.astype(jnp.float32) * gain[None, :, None]).astype(BF16)


def prepare_kernel(owner, *refs):
    sources, (gain_far, matrix), outs, picked = refs[:4], refs[4:6], refs[6:-1], refs[-1]
    experts, rows = sources[0].shape[:2]
    x, z, _ = place()
    low = lax.broadcasted_iota(jnp.int32, (rows, 128), 1) < 64
    for side in range(2):
        gate, up = (ref[...].reshape(experts * rows, 512) for ref in sources[2 * side : 2 * side + 2])
        halves = []
        for h in range(2):
            got = jnp.dot(
                gate[:, 256 * h : 256 * h + 256], matrix[h, :256, :], preferred_element_type=jnp.float32
            )
            halves.append(got + jnp.dot(
                up[:, 256 * h : 256 * h + 256], matrix[h, 256:, :], preferred_element_type=jnp.float32
            ))
        for e in range(experts):
            for pair in range(2):
                first, second = (
                    half[e * rows : (e + 1) * rows, pair * 128 : pair * 128 + 128] for half in halves
                )
                if side:
                    first, second = first * gain_far[...], second * gain_far[...]
                picked[e * 4 + 2 * pair, side] = jnp.where(low, first, second).astype(BF16)
                other = pltpu.roll(jnp.where(low, second, first), 64, 1)
                picked[e * 4 + 2 * pair + 1, side] = other.astype(BF16)
    for g, group in enumerate(GROUPS):
        for k, dz in enumerate(group):
            zt = (z + dz) % NZ
            for dx in range(NX):
                xt = (x + dx) % NX
                source = owner[xt * 2 + zt // 4] * 4 + zt % 4
                outs[g * NX + dx][k] = picked[source]
    for xt in range(NX):
        for k in range(NZ // 2):
            zt = 2 * k + z % 2
            outs[-1][xt * (NZ // 2) + k] = picked[owner[xt * 2 + zt // 4] * 4 + zt % 4]


def prepare(gate, up, gain, matrix, owner):
    rows = gate.shape[1]
    flip = [(i, i ^ 1) for i in range(2 * NX * NZ)]
    gate_far = lax.ppermute(gate, "fsdp", flip)
    up_far = lax.ppermute(up, "fsdp", flip)
    gain_far = lax.ppermute(gain, "fsdp", flip)
    shapes = [
        jax.ShapeDtypeStruct((len(group), 2, rows, 128), BF16) for group in GROUPS for _ in range(NX)
    ] + [jax.ShapeDtypeStruct((NX * NZ // 2, 2, rows, 128), BF16)]
    vmem = pl.BlockSpec(memory_space=pltpu.VMEM)
    smem = pl.BlockSpec(memory_space=pltpu.SMEM)
    outs = pl.pallas_call(
        prepare_kernel,
        out_shape=shapes,
        in_specs=[smem] + [vmem] * 6,
        out_specs=[vmem] * len(shapes),
        scratch_shapes=[
            pltpu.VMEM((16, 2, rows, 128), BF16),
        ],
        compiler_params=pltpu.CompilerParams(vmem_limit_bytes=16 * 1024 * 1024),
        name="prepare",
    )(
        owner, fold_rows(gate, gain), fold_rows(up, gain), gate_far, up_far, gain_far.reshape(rows, 1), matrix,
    )
    return [outs[g * NX : (g + 1) * NX] for g in range(len(GROUPS))], outs[-1]


def cost(megabytes):
    return pl.CostEstimate(flops=0, bytes_accessed=int(megabytes * 1e6), transcendentals=0)


def pack_kernel(outs, count, *refs):
    for out, entries in zip(refs[count:], outs):
        for at, (k, index) in enumerate(entries):
            out[at] = refs[k][index]


def pack(arrays, outs):
    vmem = pl.BlockSpec(memory_space=pltpu.VMEM)
    return pl.pallas_call(
        functools.partial(pack_kernel, outs, len(arrays)),
        out_shape=[jax.ShapeDtypeStruct((len(out),) + arrays[0].shape[1:], BF16) for out in outs],
        in_specs=[vmem] * len(arrays),
        out_specs=[vmem] * len(outs),
        compiler_params=pltpu.CompilerParams(vmem_limit_bytes=16 * 1024 * 1024),
        cost_estimate=cost(1),
        name="pack",
    )(*arrays)


def blocks_of(array, start, stop):
    return [(array, index) for index in range(start, stop)]


def place_kernel(blocks, arrays, matching, *refs):
    held = refs[:arrays]
    out, built, sems = refs[-3:]
    rows = built.shape[1]
    x, z, core = place()
    y = lax.axis_index("rep")
    saves = []
    for at, (dz, side, xs, dx, parts) in enumerate(blocks):
        for step, (k, index) in enumerate(parts):
            column = pl.multiple_of(((y + step) % NY) * 128, 128)
            built[at, :, pl.ds(column, 128)] = held[k][index]
        if dx is None:
            source = xs * NZ + (2 * dz + z % 2)
        else:
            source = (x - dx) % NX * NZ + (z - dz) % NZ
        block = matching[source * 2 + (core ^ side)]
        row = pl.multiple_of(block * rows, 16)
        save = pltpu.make_async_copy(built.at[at], out.at[pl.ds(row, rows)], sems.at[at])
        save.start()
        saves.append(save)
    for save in saves:
        save.wait()


def place_blocks(out, matching, devices, arrays, blocks):
    rows = arrays[0].shape[1]
    vmem, anywhere = pl.BlockSpec(memory_space=pltpu.VMEM), pl.BlockSpec(memory_space=pl.ANY)
    args = [matching, *arrays] + ([] if out is None else [out])
    total = len(blocks) * rows * 512 * 2
    return pl.pallas_call(
        functools.partial(place_kernel, blocks, len(arrays)),
        out_shape=jax.ShapeDtypeStruct((devices * rows, 512), BF16),
        in_specs=[pl.BlockSpec(memory_space=pltpu.SMEM)] + [vmem] * len(arrays)
        + ([] if out is None else [anywhere]),
        out_specs=anywhere,
        scratch_shapes=[
            pltpu.VMEM((len(blocks), rows, 512), BF16),
            pltpu.SemaphoreType.DMA((len(blocks),)),
        ],
        input_output_aliases={} if out is None else {len(args) - 1: 0},
        compiler_params=pltpu.CompilerParams(vmem_limit_bytes=24 * 1024 * 1024),
        cost_estimate=cost(2e-6 * total),
        name="place",
    )(*args)


def local(gate, up, norm_gain, matching, replica_slots, replica_count):
    devices = lax.axis_size("fsdp")
    rows = gate.shape[1]
    _, _, core = place()
    matrix = pick_matrix(core)
    owner = slot_owner(replica_slots, replica_count)
    parts, even = prepare(gate, up, norm_gain, matrix, owner)

    def along_x(dx):
        return [(i, ((i // 16 + dx) % NX) * 16 + i % 16) for i in range(devices)]

    def along_z(dz):
        return [(i, (i // 16) * 16 + ((i // 2 + dz) % NZ) * 2 + i % 2) for i in range(devices)]

    def along_y(dy):
        return [(i, (i + dy) % NY) for i in range(NY)]

    same_parity = [
        [(x * NZ + 2 * k + odd) * 2 + c for x in range(NX) for k in range(NZ // 2)]
        for odd in range(2) for c in range(2)
    ]

    def cross_x(g, *done):
        pieces = after(parts[g], *done)
        got = [pieces[0]] + [lax.ppermute(pieces[dx], "fsdp", along_x(dx)) for dx in range(1, NX)]
        return [jnp.stack([a[k] for a in got]).reshape(8, rows, 128) for k in range(len(GROUPS[g]))]

    def cross_z(dzs, pieces, *done):
        pieces = after(pieces, *done)
        return [lax.ppermute(p, "fsdp", along_z(dz)) for dz, p in zip(dzs, pieces)]

    def cross_y(to_right, to_left, *done):
        pair = after([jnp.concatenate(to_right), jnp.concatenate(to_left)], *done)
        return lax.ppermute(pair[0], "rep", along_y(1)), lax.ppermute(pair[1], "rep", along_y(-1))

    own1 = cross_z((1, 7), [jnp.concatenate([piece[k] for piece in parts[0]]) for k in range(2)])
    own = lax.all_to_all(even, "fsdp", 0, 0, tiled=True, axis_index_groups=same_parity)
    own = own.reshape(32, rows, 128)
    l1, r1 = cross_y(own1, own1)
    h1 = cross_y([l1[:8]], [r1[8:16]])
    le, re = cross_y([own], [own], *h1)
    bundles = []
    for dx in range(NX):
        here = [slice(8 * k + 2 * dx, 8 * k + 2 * dx + 2) for k in range(2)]
        bundle = [own1[k][here[0]] for k in range(2)] + [r1[h] for h in here]
        bundle += [h1[0][here[0]], h1[1][here[0]]] + [l1[h] for h in here]
        bundle = jnp.concatenate(bundle)
        bundles.append(lax.ppermute(bundle, "fsdp", along_x(dx)) if dx else bundle)
    own3 = cross_z((3, 5), cross_x(1, *own1))
    l3, r3 = cross_y(own3 + [le[:16]], own3 + [re[16:]])
    l4, r4 = cross_y([l3[:8]], [r3[8:16]])
    late = [
        (dz, side, None, dx, tuple((dx, step * 4 + 2 * k + side) for step in range(NY)))
        for dx in range(NX) for k, dz in enumerate(GROUPS[0]) for side in range(2)
    ]
    evens = [
        (at // 2 % 4, at % 2, at // 8, None, ((0, at), (2, at), (3, 16 + at) if at < 16 else (4, at), (1, at)))
        for at in range(32)
    ]
    out = place_blocks(None, matching, devices, [own, le, re, l3, r3], evens)
    out = place_blocks(out, matching, devices, bundles, late)
    odds = [
        (GROUPS[1][at // 8], at % 2, None, at % 8 // 2,
         ((at // 8, at % 8), (3, at), (4, at) if at < 8 else (5, at - 8), (2, at)))
        for at in range(16)
    ]
    out = place_blocks(out, matching, devices, [*own3, l3, r3, l4, r4], odds)
    return out[None]


def solution(mesh):
    return jax.shard_map(
        local,
        mesh=mesh,
        in_specs=(P(None, "fsdp", "rep"), P(None, "fsdp", "rep"), P("fsdp"), P(), P(), P()),
        out_specs=P("fsdp", None, None),
        check_vma=False,
    )
```

```python
import functools

import jax
import jax.numpy as jnp
from jax import lax
from jax.experimental import pallas as pl
from jax.experimental.pallas import tpu as pltpu
from jax.sharding import PartitionSpec as P

NX, NZ, NY = 4, 8, 4
SLOTS, BLOCKS = 8, 8
GROUPS = ((1, 7), (3, 5))
BF16 = jnp.bfloat16


def place():
    me = lax.axis_index("fsdp")
    return me // (2 * NZ), (me // 2) % NZ, me % 2


def after(arrays, *done):
    return lax.optimization_barrier((list(arrays), done))[0]


def slot_owner(replica_slots, replica_count):
    shape = (SLOTS,) + replica_slots.shape
    slot, expert, place_in_list = (lax.broadcasted_iota(jnp.int32, shape, k) for k in range(3))
    live = jnp.clip(replica_count[None, :, None] - place_in_list, 0, 1)
    return jnp.sum(jnp.where(replica_slots[None] == slot, live * expert, 0), axis=(1, 2))


def pick_matrix(core):
    shape = (2, 512, 256)
    half, row, column = (lax.broadcasted_iota(jnp.int32, shape, k) for k in range(3))
    lane = column % 64
    residue = (column // 64) ^ half
    wanted = (lane % 2) * 256 + 8 * (lane // 2) + 2 * residue + core
    return (row == wanted).astype(BF16)


def fold_rows(weights, gain):
    return (weights.astype(jnp.float32) * gain[None, :, None]).astype(BF16)


def prepare_kernel(owner, *refs):
    sources, (gain_far, matrix), outs, picked = refs[:4], refs[4:6], refs[6:-1], refs[-1]
    experts, rows = sources[0].shape[:2]
    x, z, _ = place()
    low = lax.broadcasted_iota(jnp.int32, (rows, 128), 1) < 64
    for side in range(2):
        gate, up = (ref[...].reshape(experts * rows, 512) for ref in sources[2 * side : 2 * side + 2])
        halves = []
        for h in range(2):
            got = jnp.dot(
                gate[:, 256 * h : 256 * h + 256], matrix[h, :256, :], preferred_element_type=jnp.float32
            )
            halves.append(got + jnp.dot(
                up[:, 256 * h : 256 * h + 256], matrix[h, 256:, :], preferred_element_type=jnp.float32
            ))
        for e in range(experts):
            for pair in range(2):
                first, second = (
                    half[e * rows : (e + 1) * rows, pair * 128 : pair * 128 + 128] for half in halves
                )
                if side:
                    first, second = first * gain_far[...], second * gain_far[...]
                picked[e * 4 + 2 * pair, side] = jnp.where(low, first, second).astype(BF16)
                other = pltpu.roll(jnp.where(low, second, first), 64, 1)
                picked[e * 4 + 2 * pair + 1, side] = other.astype(BF16)
    for g, group in enumerate(GROUPS):
        for k, dz in enumerate(group):
            zt = (z + dz) % NZ
            for dx in range(NX):
                xt = (x + dx) % NX
                source = owner[xt * 2 + zt // 4] * 4 + zt % 4
                outs[g * NX + dx][k] = picked[source]
    for xt in range(NX):
        for k in range(NZ // 2):
            zt = 2 * k + z % 2
            outs[-1][xt * (NZ // 2) + k] = picked[owner[xt * 2 + zt // 4] * 4 + zt % 4]


def prepare(gate, up, gain, matrix, owner):
    rows = gate.shape[1]
    flip = [(i, i ^ 1) for i in range(2 * NX * NZ)]
    gate_far = lax.ppermute(gate, "fsdp", flip)
    up_far = lax.ppermute(up, "fsdp", flip)
    gain_far = lax.ppermute(gain, "fsdp", flip)
    shapes = [
        jax.ShapeDtypeStruct((len(group), 2, rows, 128), BF16) for group in GROUPS for _ in range(NX)
    ] + [jax.ShapeDtypeStruct((NX * NZ // 2, 2, rows, 128), BF16)]
    vmem = pl.BlockSpec(memory_space=pltpu.VMEM)
    smem = pl.BlockSpec(memory_space=pltpu.SMEM)
    outs = pl.pallas_call(
        prepare_kernel,
        out_shape=shapes,
        in_specs=[smem] + [vmem] * 6,
        out_specs=[vmem] * len(shapes),
        scratch_shapes=[
            pltpu.VMEM((16, 2, rows, 128), BF16),
        ],
        compiler_params=pltpu.CompilerParams(vmem_limit_bytes=16 * 1024 * 1024),
        name="prepare",
    )(
        owner, fold_rows(gate, gain), fold_rows(up, gain), gate_far, up_far, gain_far.reshape(rows, 1), matrix,
    )
    return [outs[g * NX : (g + 1) * NX] for g in range(len(GROUPS))], outs[-1]


def cost(megabytes):
    return pl.CostEstimate(flops=0, bytes_accessed=int(megabytes * 1e6), transcendentals=0)


def pack_kernel(outs, count, *refs):
    for out, entries in zip(refs[count:], outs):
        for at, (k, index) in enumerate(entries):
            out[at] = refs[k][index]


def pack(arrays, outs):
    vmem = pl.BlockSpec(memory_space=pltpu.VMEM)
    return pl.pallas_call(
        functools.partial(pack_kernel, outs, len(arrays)),
        out_shape=[jax.ShapeDtypeStruct((len(out),) + arrays[0].shape[1:], BF16) for out in outs],
        in_specs=[vmem] * len(arrays),
        out_specs=[vmem] * len(outs),
        compiler_params=pltpu.CompilerParams(vmem_limit_bytes=16 * 1024 * 1024),
        cost_estimate=cost(1),
        name="pack",
    )(*arrays)


def blocks_of(array, start, stop):
    return [(array, index) for index in range(start, stop)]


def place_kernel(blocks, arrays, matching, *refs):
    held = refs[:arrays]
    out, built, sems = refs[-3:]
    rows = built.shape[1]
    x, z, core = place()
    y = lax.axis_index("rep")
    saves = []
    for at, (dz, side, xs, dx, parts) in enumerate(blocks):
        for step, (k, index) in enumerate(parts):
            column = pl.multiple_of(((y + step) % NY) * 128, 128)
            built[at, :, pl.ds(column, 128)] = held[k][index]
        if dx is None:
            source = xs * NZ + (2 * dz + z % 2)
        else:
            source = (x - dx) % NX * NZ + (z - dz) % NZ
        block = matching[source * 2 + (core ^ side)]
        row = pl.multiple_of(block * rows, 16)
        save = pltpu.make_async_copy(built.at[at], out.at[pl.ds(row, rows)], sems.at[at])
        save.start()
        saves.append(save)
    for save in saves:
        save.wait()


def place_blocks(out, matching, devices, arrays, blocks):
    rows = arrays[0].shape[1]
    vmem, anywhere = pl.BlockSpec(memory_space=pltpu.VMEM), pl.BlockSpec(memory_space=pl.ANY)
    args = [matching, *arrays] + ([] if out is None else [out])
    total = len(blocks) * rows * 512 * 2
    return pl.pallas_call(
        functools.partial(place_kernel, blocks, len(arrays)),
        out_shape=jax.ShapeDtypeStruct((devices * rows, 512), BF16),
        in_specs=[pl.BlockSpec(memory_space=pltpu.SMEM)] + [vmem] * len(arrays)
        + ([] if out is None else [anywhere]),
        out_specs=anywhere,
        scratch_shapes=[
            pltpu.VMEM((len(blocks), rows, 512), BF16),
            pltpu.SemaphoreType.DMA((len(blocks),)),
        ],
        input_output_aliases={} if out is None else {len(args) - 1: 0},
        compiler_params=pltpu.CompilerParams(vmem_limit_bytes=24 * 1024 * 1024),
        cost_estimate=cost(2e-6 * total),
        name="place",
    )(*args)


def local(gate, up, norm_gain, matching, replica_slots, replica_count):
    devices = lax.axis_size("fsdp")
    rows = gate.shape[1]
    _, _, core = place()
    matrix = pick_matrix(core)
    owner = slot_owner(replica_slots, replica_count)
    parts, even = prepare(gate, up, norm_gain, matrix, owner)

    def along_x(dx):
        return [(i, ((i // 16 + dx) % NX) * 16 + i % 16) for i in range(devices)]

    def along_z(dz):
        return [(i, (i // 16) * 16 + ((i // 2 + dz) % NZ) * 2 + i % 2) for i in range(devices)]

    def along_y(dy):
        return [(i, (i + dy) % NY) for i in range(NY)]

    same_parity = [
        [(x * NZ + 2 * k + odd) * 2 + c for x in range(NX) for k in range(NZ // 2)]
        for odd in range(2) for c in range(2)
    ]

    def cross_x(g, *done):
        pieces = after(parts[g], *done)
        got = [pieces[0]] + [lax.ppermute(pieces[dx], "fsdp", along_x(dx)) for dx in range(1, NX)]
        return [jnp.stack([a[k] for a in got]).reshape(8, rows, 128) for k in range(len(GROUPS[g]))]

    def cross_z(dzs, pieces, *done):
        pieces = after(pieces, *done)
        return [lax.ppermute(p, "fsdp", along_z(dz)) for dz, p in zip(dzs, pieces)]

    def cross_y(to_right, to_left, *done):
        pair = after([jnp.concatenate(to_right), jnp.concatenate(to_left)], *done)
        return lax.ppermute(pair[0], "rep", along_y(1)), lax.ppermute(pair[1], "rep", along_y(-1))

    own1 = cross_z((1, 7), [jnp.concatenate([piece[k] for piece in parts[0]]) for k in range(2)])
    own = lax.all_to_all(even, "fsdp", 0, 0, tiled=True, axis_index_groups=same_parity)
    own = own.reshape(32, rows, 128)
    l1, r1 = cross_y(own1, own1)
    h1 = cross_y([l1[:8]], [r1[8:16]])
    le, re = cross_y([own], [own], *h1)
    bundles = []
    for dx in range(NX):
        here = [slice(8 * k + 2 * dx, 8 * k + 2 * dx + 2) for k in range(2)]
        bundle = [own1[k][here[0]] for k in range(2)] + [r1[h] for h in here]
        bundle += [h1[0][here[0]], h1[1][here[0]]] + [l1[h] for h in here]
        bundle = jnp.concatenate(bundle)
        bundles.append(lax.ppermute(bundle, "fsdp", along_x(dx)) if dx else bundle)
    own3 = cross_z((3, 5), cross_x(1, *h1))
    l3, r3 = cross_y(own3 + [le[:16]], own3 + [re[16:]])
    l4, r4 = cross_y([l3[:8]], [r3[8:16]])
    late = [
        (dz, side, None, dx, tuple((dx, step * 4 + 2 * k + side) for step in range(NY)))
        for dx in range(NX) for k, dz in enumerate(GROUPS[0]) for side in range(2)
    ]
    evens = [
        (at // 2 % 4, at % 2, at // 8, None, ((0, at), (2, at), (3, 16 + at) if at < 16 else (4, at), (1, at)))
        for at in range(32)
    ]
    out = place_blocks(None, matching, devices, [own, le, re, l3, r3], evens)
    out = place_blocks(out, matching, devices, bundles, late)
    odds = [
        (GROUPS[1][at // 8], at % 2, None, at % 8 // 2,
         ((at // 8, at % 8), (3, at), (4, at) if at < 8 else (5, at - 8), (2, at)))
        for at in range(16)
    ]
    out = place_blocks(out, matching, devices, [*own3, l3, r3, l4, r4], odds)
    return out[None]


def solution(mesh):
    return jax.shard_map(
        local,
        mesh=mesh,
        in_specs=(P(None, "fsdp", "rep"), P(None, "fsdp", "rep"), P("fsdp"), P(), P(), P()),
        out_specs=P("fsdp", None, None),
        check_vma=False,
    )
```

```python
import functools

import jax
import jax.numpy as jnp
from jax import lax
from jax.experimental import pallas as pl
from jax.experimental.pallas import tpu as pltpu
from jax.sharding import PartitionSpec as P

NX, NZ, NY = 4, 8, 4
SLOTS, BLOCKS = 8, 8
GROUPS = ((1, 7), (3, 5))
BF16 = jnp.bfloat16


def place():
    me = lax.axis_index("fsdp")
    return me // (2 * NZ), (me // 2) % NZ, me % 2


def after(arrays, *done):
    return lax.optimization_barrier((list(arrays), done))[0]


def slot_owner(replica_slots, replica_count):
    shape = (SLOTS,) + replica_slots.shape
    slot, expert, place_in_list = (lax.broadcasted_iota(jnp.int32, shape, k) for k in range(3))
    live = jnp.clip(replica_count[None, :, None] - place_in_list, 0, 1)
    return jnp.sum(jnp.where(replica_slots[None] == slot, live * expert, 0), axis=(1, 2))


def pick_matrix(core):
    shape = (2, 512, 256)
    half, row, column = (lax.broadcasted_iota(jnp.int32, shape, k) for k in range(3))
    lane = column % 64
    residue = (column // 64) ^ half
    wanted = (lane % 2) * 256 + 8 * (lane // 2) + 2 * residue + core
    return (row == wanted).astype(BF16)


def fold_rows(weights, gain):
    return (weights.astype(jnp.float32) * gain[None, :, None]).astype(BF16)


def prepare_kernel(owner, *refs):
    sources, (gain_far, matrix), outs, picked = refs[:4], refs[4:6], refs[6:-1], refs[-1]
    experts, rows = sources[0].shape[:2]
    x, z, _ = place()
    low = lax.broadcasted_iota(jnp.int32, (rows, 128), 1) < 64
    for side in range(2):
        gate, up = (ref[...].reshape(experts * rows, 512) for ref in sources[2 * side : 2 * side + 2])
        halves = []
        for h in range(2):
            got = jnp.dot(
                gate[:, 256 * h : 256 * h + 256], matrix[h, :256, :], preferred_element_type=jnp.float32
            )
            halves.append(got + jnp.dot(
                up[:, 256 * h : 256 * h + 256], matrix[h, 256:, :], preferred_element_type=jnp.float32
            ))
        for e in range(experts):
            for pair in range(2):
                first, second = (
                    half[e * rows : (e + 1) * rows, pair * 128 : pair * 128 + 128] for half in halves
                )
                if side:
                    first, second = first * gain_far[...], second * gain_far[...]
                picked[e * 4 + 2 * pair, side] = jnp.where(low, first, second).astype(BF16)
                other = pltpu.roll(jnp.where(low, second, first), 64, 1)
                picked[e * 4 + 2 * pair + 1, side] = other.astype(BF16)
    for g, group in enumerate(GROUPS):
        for k, dz in enumerate(group):
            zt = (z + dz) % NZ
            for dx in range(NX):
                xt = (x + dx) % NX
                source = owner[xt * 2 + zt // 4] * 4 + zt % 4
                outs[g * NX + dx][k] = picked[source]
    for xt in range(NX):
        for k in range(NZ // 2):
            zt = 2 * k + z % 2
            outs[-1][xt * (NZ // 2) + k] = picked[owner[xt * 2 + zt // 4] * 4 + zt % 4]


def prepare(gate, up, gain, matrix, owner):
    rows = gate.shape[1]
    flip = [(i, i ^ 1) for i in range(2 * NX * NZ)]
    gate_far = lax.ppermute(gate, "fsdp", flip)
    up_far = lax.ppermute(up, "fsdp", flip)
    gain_far = lax.ppermute(gain, "fsdp", flip)
    shapes = [
        jax.ShapeDtypeStruct((len(group), 2, rows, 128), BF16) for group in GROUPS for _ in range(NX)
    ] + [jax.ShapeDtypeStruct((NX * NZ // 2, 2, rows, 128), BF16)]
    vmem = pl.BlockSpec(memory_space=pltpu.VMEM)
    smem = pl.BlockSpec(memory_space=pltpu.SMEM)
    outs = pl.pallas_call(
        prepare_kernel,
        out_shape=shapes,
        in_specs=[smem] + [vmem] * 6,
        out_specs=[vmem] * len(shapes),
        scratch_shapes=[
            pltpu.VMEM((16, 2, rows, 128), BF16),
        ],
        compiler_params=pltpu.CompilerParams(vmem_limit_bytes=16 * 1024 * 1024),
        name="prepare",
    )(
        owner, fold_rows(gate, gain), fold_rows(up, gain), gate_far, up_far, gain_far.reshape(rows, 1), matrix,
    )
    return [outs[g * NX : (g + 1) * NX] for g in range(len(GROUPS))], outs[-1]


def cost(megabytes):
    return pl.CostEstimate(flops=0, bytes_accessed=int(megabytes * 1e6), transcendentals=0)


def pack_kernel(outs, count, *refs):
    for out, entries in zip(refs[count:], outs):
        for at, (k, index) in enumerate(entries):
            out[at] = refs[k][index]


def pack(arrays, outs):
    vmem = pl.BlockSpec(memory_space=pltpu.VMEM)
    return pl.pallas_call(
        functools.partial(pack_kernel, outs, len(arrays)),
        out_shape=[jax.ShapeDtypeStruct((len(out),) + arrays[0].shape[1:], BF16) for out in outs],
        in_specs=[vmem] * len(arrays),
        out_specs=[vmem] * len(outs),
        compiler_params=pltpu.CompilerParams(vmem_limit_bytes=16 * 1024 * 1024),
        cost_estimate=cost(1),
        name="pack",
    )(*arrays)


def blocks_of(array, start, stop):
    return [(array, index) for index in range(start, stop)]


def place_kernel(blocks, arrays, matching, *refs):
    held = refs[:arrays]
    out, built, sems = refs[-3:]
    rows = built.shape[1]
    x, z, core = place()
    y = lax.axis_index("rep")
    saves = []
    for at, (dz, side, xs, dx, parts) in enumerate(blocks):
        for step, (k, index) in enumerate(parts):
            column = pl.multiple_of(((y + step) % NY) * 128, 128)
            built[at, :, pl.ds(column, 128)] = held[k][index]
        if dx is None:
            source = xs * NZ + (2 * dz + z % 2)
        else:
            source = (x - dx) % NX * NZ + (z - dz) % NZ
        block = matching[source * 2 + (core ^ side)]
        row = pl.multiple_of(block * rows, 16)
        save = pltpu.make_async_copy(built.at[at], out.at[pl.ds(row, rows)], sems.at[at])
        save.start()
        saves.append(save)
    for save in saves:
        save.wait()


def place_blocks(out, matching, devices, arrays, blocks):
    rows = arrays[0].shape[1]
    vmem, anywhere = pl.BlockSpec(memory_space=pltpu.VMEM), pl.BlockSpec(memory_space=pl.ANY)
    args = [matching, *arrays] + ([] if out is None else [out])
    total = len(blocks) * rows * 512 * 2
    return pl.pallas_call(
        functools.partial(place_kernel, blocks, len(arrays)),
        out_shape=jax.ShapeDtypeStruct((devices * rows, 512), BF16),
        in_specs=[pl.BlockSpec(memory_space=pltpu.SMEM)] + [vmem] * len(arrays)
        + ([] if out is None else [anywhere]),
        out_specs=anywhere,
        scratch_shapes=[
            pltpu.VMEM((len(blocks), rows, 512), BF16),
            pltpu.SemaphoreType.DMA((len(blocks),)),
        ],
        input_output_aliases={} if out is None else {len(args) - 1: 0},
        compiler_params=pltpu.CompilerParams(vmem_limit_bytes=24 * 1024 * 1024),
        cost_estimate=cost(2e-6 * total),
        name="place",
    )(*args)


def local(gate, up, norm_gain, matching, replica_slots, replica_count):
    devices = lax.axis_size("fsdp")
    rows = gate.shape[1]
    _, _, core = place()
    matrix = pick_matrix(core)
    owner = slot_owner(replica_slots, replica_count)
    parts, even = prepare(gate, up, norm_gain, matrix, owner)

    def along_x(dx):
        return [(i, ((i // 16 + dx) % NX) * 16 + i % 16) for i in range(devices)]

    def along_z(dz):
        return [(i, (i // 16) * 16 + ((i // 2 + dz) % NZ) * 2 + i % 2) for i in range(devices)]

    def along_y(dy):
        return [(i, (i + dy) % NY) for i in range(NY)]

    same_parity = [
        [(x * NZ + 2 * k + odd) * 2 + c for x in range(NX) for k in range(NZ // 2)]
        for odd in range(2) for c in range(2)
    ]

    def cross_x(g, *done):
        pieces = after(parts[g], *done)
        got = [pieces[0]] + [lax.ppermute(pieces[dx], "fsdp", along_x(dx)) for dx in range(1, NX)]
        return [jnp.stack([a[k] for a in got]).reshape(8, rows, 128) for k in range(len(GROUPS[g]))]

    def cross_z(dzs, pieces, *done):
        pieces = after(pieces, *done)
        return [lax.ppermute(p, "fsdp", along_z(dz)) for dz, p in zip(dzs, pieces)]

    def cross_y(to_right, to_left, *done):
        pair = after([jnp.concatenate(to_right), jnp.concatenate(to_left)], *done)
        return lax.ppermute(pair[0], "rep", along_y(1)), lax.ppermute(pair[1], "rep", along_y(-1))

    own1 = cross_z((1, 7), [jnp.concatenate([piece[k] for piece in parts[0]]) for k in range(2)])
    own = lax.all_to_all(even, "fsdp", 0, 0, tiled=True, axis_index_groups=same_parity)
    own = own.reshape(32, rows, 128)
    l1, r1 = cross_y(own1, own1)
    h1 = cross_y([l1[:8]], [r1[8:16]])
    le, re = cross_y([own], [own], *h1)
    bundles = []
    for dx in range(NX):
        here = [slice(8 * k + 2 * dx, 8 * k + 2 * dx + 2) for k in range(2)]
        bundle = [own1[k][here[0]] for k in range(2)] + [r1[h] for h in here]
        bundle += [h1[0][here[0]], h1[1][here[0]]] + [l1[h] for h in here]
        bundle = jnp.concatenate(bundle)
        bundles.append(lax.ppermute(bundle, "fsdp", along_x(dx)) if dx else bundle)
    own3 = cross_z((3, 5), cross_x(1, *own1))
    l3, r3 = cross_y(own3 + [le[:16]], own3 + [re[16:]])
    l4, r4 = cross_y([l3[:8]], [r3[8:16]])
    late = [
        (dz, side, None, dx, tuple((dx, step * 4 + 2 * k + side) for step in range(NY)))
        for dx in range(NX) for k, dz in enumerate(GROUPS[0]) for side in range(2)
    ]
    evens = [
        (at // 2 % 4, at % 2, at // 8, None, ((0, at), (2, at), (3, 16 + at) if at < 16 else (4, at), (1, at)))
        for at in range(32)
    ]
    out = place_blocks(None, matching, devices, [own, le, re, l3, r3], evens)
    odds = [
        (GROUPS[1][at // 8], at % 2, None, at % 8 // 2,
         ((at // 8, at % 8), (3, at), (4, at) if at < 8 else (5, at - 8), (2, at)))
        for at in range(16)
    ]
    late = [(dz, side, xs, dx, tuple((k + 6, at) for k, at in parts)) for dz, side, xs, dx, parts in late]
    out = place_blocks(out, matching, devices, [*own3, l3, r3, l4, r4, *bundles], late + odds)
    return out[None]


def solution(mesh):
    return jax.shard_map(
        local,
        mesh=mesh,
        in_specs=(P(None, "fsdp", "rep"), P(None, "fsdp", "rep"), P("fsdp"), P(), P(), P()),
        out_specs=P("fsdp", None, None),
        check_vma=False,
    )
```
